32 devices in a mesh: win: 4 (over x, core), seq: 8 (over z, y).
Axes of the slice: x: 2, y: 2, z: 4, core: 2. Of those that a mesh axis runs over, the one named last changes fastest.
Arguments:
- embedded: bfloat16 [4, 8192, 768], P('win', 'seq'), may hold values from -6 to 6
- lengths: int32 [4, 4], P('win'), may hold values from 1 to 4096, 8192 in all within a row
- norm_gains: bfloat16 [8, 768], replicated, may hold values from 0.5 to 1.5
- biases: bfloat16 [8, 768], replicated, may hold values from -3 to 3
- conv_taps: bfloat16 [8, 3, 768], replicated, may hold values from -3 to 3
- pointwise: bfloat16 [8, 768, 192], replicated, may hold values from -0.4375 to 0.4375
- channel_order: int32 [8, 768], replicated, may hold values from 0 to 767, each once within a row
Outputs:
- encoded: bfloat16 [4, 8192, 768], P('win', 'seq')
The draws below stay inside these ranges and needn't reach their ends.
Inputs may be any that keep to these rules, and one draw needn't show every extreme that they name: The lengths of each pack sum to 8192, and some window of each pack has exactly 4096 bins. `channel_order`: each row is a permutation of the 768 channels.
All inputs are finite; a program needn't handle non-finite values.
Results may differ from the reference program's by a relative error of at most 0.015.
Values may be sent and summed in bfloat16 or wider, within the bound.
A program may use at most 64 MiB of HBM per device.

```python
import math
import jax
import jax.numpy as jnp
import numpy as np
from jax import lax

C = 768
GROUPS = 4
CG = 192
LAYERS = 8
BIN_DEV = 1024
PACKS = 4
BINS = 8192
WINS = 4
WIN_MOST = 4096


def draw_embedded(key, part):
    key = jax.random.fold_in(key, 7)
    noise_key, column_key, row_key = jax.random.split(key, 3)
    column_scale = jnp.exp(jax.random.uniform(column_key, (1, 1, C), jnp.float32, math.log(0.3), math.log(3.0)))
    row_scale = jnp.exp(jax.random.uniform(row_key, (PACKS, BINS, 1), jnp.float32, math.log(0.4), math.log(2.5)))
    sample = jax.random.normal(noise_key, (PACKS, BINS, C), jnp.float32)
    return jnp.clip(0.5 * sample * row_scale * column_scale, -6.0, 6.0).astype(jnp.bfloat16)


def profile(number_of, total, bound, skew):
    weights = [(1 << 20) // math.isqrt(grade ** skew) + 1 for grade in range(2, number_of + 1)]
    surplus, counts = total - bound - (number_of - 1), [1] * (number_of - 1)
    while surplus > 0:
        free = [i for i in range(number_of - 1) if counts[i] < bound]
        mass, left = sum([weights[i] for i in free]), surplus
        for i in free:
            addition = min(bound - counts[i], max(1, left * weights[i] // mass), surplus)
            counts[i] = counts[i] + addition
            surplus = surplus - addition
    return np.array([bound] + counts)


def uneven_parts(rng, count, total, reach, slope):
    if count == 2:
        one = jax.random.randint(rng, (), max(1, total - reach), min(reach, total - 1) + 1)
        return jnp.stack([one, total - one])
    tallies = jnp.asarray(profile(count, total, reach, slope), jnp.int32)
    twos = (count - 1) // 2
    giver, taker = tallies[1:1 + 2 * twos:2], tallies[2:2 + 2 * twos:2]
    slack = jnp.minimum(giver - 1, reach - taker)
    shifted = jax.random.randint(jax.random.fold_in(rng, 1), (twos,), 0, 1 << 20) % (slack + 1)
    tallies = tallies.at[1:1 + 2 * twos:2].set(giver - shifted).at[2:2 + 2 * twos:2].set(taker + shifted)
    return tallies[jax.random.permutation(jax.random.fold_in(rng, 2), count)]


def scatter_about(own_key, dims, deviation, limit, held_as=jnp.bfloat16):
    drawn = jax.random.normal(own_key, dims, jnp.float32) * deviation
    return jnp.minimum(jnp.maximum(drawn, -limit), limit).astype(held_as)


def setup_inputs(seed: int = 0) -> dict:
    keys = jax.random.split(jax.random.key(seed), 8)
    return {
        "embedded": draw_embedded(jax.random.fold_in(keys[7], 71), 0),
        "lengths": jax.vmap(lambda own: uneven_parts(own, WINS, BINS, WIN_MOST, 2))(jax.random.split(keys[1], PACKS)).reshape((PACKS, WINS)).astype(jnp.int32),
        "norm_gains": jnp.clip(1.0 + 0.1 * jax.random.normal(keys[2], (LAYERS, C), jnp.float32), 0.5, 1.5).astype(jnp.bfloat16),
        "biases": scatter_about(keys[3], (LAYERS, C), 0.5, 3.0),
        "conv_taps": scatter_about(keys[4], (LAYERS, 3, C), 0.6, 3.0),
        "pointwise": scatter_about(keys[5], (LAYERS, C, CG), CG ** -0.5, 0.4375),
        "channel_order": jax.vmap(lambda own: jax.random.permutation(own, C))(jax.random.split(keys[6], LAYERS)).reshape((LAYERS, C)).astype(jnp.int32),
    }


epsilon = 1e-06

def window_bounds(lengths, positions):
    window_ends = jnp.cumsum(lengths, axis=-1).astype(jnp.int32)
    passed = window_ends[..., None, :] <= positions[:, None]
    starts = lax.optimization_barrier(jnp.max(jnp.where(passed, window_ends[..., None, :], 0), axis=-1)).astype(jnp.int32)
    last_end = window_ends[..., -1:][..., None, :]
    window_stops = lax.optimization_barrier(jnp.min(jnp.where(passed, last_end, window_ends[..., None, :]), axis=-1)).astype(jnp.int32)
    return (starts, window_stops)

def normalise(stream, gain_row):
    stream_f32 = stream.astype(jnp.float32)
    inverse_rms = lax.rsqrt(lax.optimization_barrier(jnp.mean(stream_f32 * stream_f32, axis=-1, keepdims=True)) + epsilon)
    return (stream_f32 * inverse_rms * gain_row.astype(jnp.float32)).astype(jnp.bfloat16)

def finish(stream, normed, earlier, later_rows, left_valid, right_valid, bias_row, kernel, weight_block, order_row):
    kernel_f32 = kernel.astype(jnp.float32)
    mixed_sum = kernel_f32[0] * jnp.where(left_valid[..., None], earlier.astype(jnp.float32), 0.0)
    mixed_sum = mixed_sum + kernel_f32[1] * normed.astype(jnp.float32)
    mixed_sum = mixed_sum + kernel_f32[2] * jnp.where(right_valid[..., None], later_rows.astype(jnp.float32), 0.0)
    mixed_sum = mixed_sum + bias_row.astype(jnp.float32)
    activated = jax.nn.gelu(mixed_sum, approximate=True).astype(jnp.bfloat16)
    grouped = activated.reshape(BINS, GROUPS, CG).astype(jnp.float32)
    blocks = weight_block.reshape(GROUPS, CG, CG).astype(jnp.float32)
    projected = jnp.einsum('ngi,gio->ngo', grouped, blocks, precision=lax.Precision.HIGHEST).reshape(BINS, C)
    shuffled = jnp.take(projected, order_row, axis=-1)
    return (stream.astype(jnp.float32) + shuffled).astype(jnp.bfloat16)

def reference(embedded, lengths, norm_gains, biases, conv_taps, pointwise, channel_order):

    def one_pack(inputs):
        stream, pack_lengths = inputs
        positions = jnp.arange(BINS, dtype=jnp.int32)
        starts, window_stops = window_bounds(pack_lengths, positions)
        for layer_id in range(LAYERS):
            dilation = BIN_DEV * 2 ** layer_id // 2 ** (LAYERS - 2)
            normed = normalise(stream, norm_gains[layer_id])
            blank = jnp.zeros((dilation, C), jnp.bfloat16)
            earlier = jnp.concatenate([blank, normed[:-dilation]], axis=0)
            later_rows = jnp.concatenate([normed[dilation:], blank], axis=0)
            stream = finish(stream, normed, earlier, later_rows, positions - dilation >= starts, positions + dilation < window_stops, biases[layer_id], conv_taps[layer_id], pointwise[layer_id], channel_order[layer_id])
        return stream
    return lax.map(one_pack, (embedded, lengths))
```

```python
import functools

import jax
import jax.numpy as jnp
from jax import lax
from jax.experimental import pallas as pl
from jax.experimental.pallas import tpu as pltpu
from jax.sharding import PartitionSpec as P

epsilon = 1e-06
LANES = 128
CHUNK = 128
MXU_ROWS = 256
GELU_C = 0.7978845608028654


def build_weights(pw_ref, order_ref, w_ref, layers):
    channels = w_ref.shape[-1]
    width = pw_ref.shape[-1]

    @pl.loop(0, len(layers))
    def _(i):
        layer = i + layers[0]
        order = order_ref[layer]
        for g in range(channels // width):
            out_ids = lax.broadcasted_iota(jnp.int32, (width, channels), 0) + g * width
            one_hot = jnp.where(out_ids == order, 1.0, 0.0).astype(jnp.bfloat16)
            rows = slice(g * width, (g + 1) * width)
            w_ref[i, rows, :] = jnp.dot(
                pw_ref[layer, rows, :], one_hot, preferred_element_type=jnp.float32
            ).astype(jnp.bfloat16)


def window_rows(len_ref, lo_ref, hi_ref, residue, modulus):
    rows = lo_ref.shape[0]
    pos = lax.broadcasted_iota(jnp.int32, (rows, LANES), 0) * modulus + residue
    wins = len_ref.shape[1]
    total = jnp.int32(0)
    for k in range(wins):
        total = total + len_ref[0, k]
    lo = jnp.zeros((rows, LANES), jnp.int32)
    hi = jnp.zeros((rows, LANES), jnp.int32) + total
    end = jnp.int32(0)
    ends = []
    for k in range(wins):
        end = end + len_ref[0, k]
        ends.append(end)
    for end in ends:
        lo = jnp.where(pos >= end, end, lo)
    for end in reversed(ends):
        hi = jnp.where(pos < end, end, hi)
    lo_ref[...] = pos - lo
    hi_ref[...] = hi - pos


def put_unit(u_ref, pad, start, size, stream):
    mean = jnp.mean(stream * stream, axis=-1, keepdims=True)
    u_ref[pl.ds(pad + start, size), :] = stream * lax.rsqrt(mean + epsilon)


def run_layers(x_ref, y_ref, gain_ref, bias_ref, taps_ref, w_ref, u_ref, act_ref, lo_ref, hi_ref, layers, shifts, modulus):
    rows, channels = x_ref.shape
    pad = (u_ref.shape[0] - rows) // 2
    big = min(MXU_ROWS, rows)

    @pl.loop(0, rows // big)
    def _(i):
        start = pl.multiple_of(i * big, big)
        put_unit(u_ref, pad, start, big, x_ref[pl.ds(start, big), :].astype(jnp.float32))

    for i, layer in enumerate(layers):
        shift = shifts[i]
        source = x_ref if i == 0 else y_ref

        def mix(j, shift=shift, layer=layer):
            at = (lambda n: n) if isinstance(j, int) else (lambda n: pl.multiple_of(n, 8))
            start = j * CHUNK if isinstance(j, int) else pl.multiple_of(j * CHUNK, CHUNK)
            here = pl.ds(start, CHUNK)
            left_ok = lo_ref[here, :] >= shift * modulus
            right_ok = hi_ref[here, :] > shift * modulus
            for k in range(channels // LANES):
                cols = slice(k * LANES, (k + 1) * LANES)
                gain = gain_ref[layer : layer + 1, cols].astype(jnp.float32)
                tap = [gain * taps_ref[layer, t : t + 1, cols].astype(jnp.float32) for t in range(3)]
                bias = bias_ref[layer : layer + 1, cols].astype(jnp.float32)
                v = tap[1] * u_ref[pl.ds(at(start + pad), CHUNK), cols] + bias
                v = v + tap[0] * jnp.where(left_ok, u_ref[pl.ds(at(start + (pad - shift)), CHUNK), cols], 0.0)
                v = v + tap[2] * jnp.where(right_ok, u_ref[pl.ds(at(start + (pad + shift)), CHUNK), cols], 0.0)
                inner = v * (GELU_C + (GELU_C * 0.044715) * (v * v))
                half = 0.5 * v
                act_ref[here, cols] = (half + half * jnp.tanh(inner)).astype(jnp.bfloat16)

        if shift % 8:
            for j in range(rows // CHUNK):
                mix(j)
        else:
            pl.loop(0, rows // CHUNK)(mix)

        @pl.loop(0, rows // big)
        def _(j):
            start = pl.multiple_of(j * big, big)
            here = pl.ds(start, big)
            projected = jnp.dot(act_ref[here, :], w_ref[i], preferred_element_type=jnp.float32)
            fresh = (source[here, :].astype(jnp.float32) + projected).astype(jnp.bfloat16)
            y_ref[here, :] = fresh
            if i + 1 < len(layers):
                put_unit(u_ref, pad, start, big, fresh.astype(jnp.float32))


def stack_kernel(layers, shifts, modulus, held, len_ref, x_ref, gain_ref, bias_ref, taps_ref, pw_ref, order_ref, y_ref, w_ref, u_ref, act_ref, lo_ref, hi_ref):
    h = pl.program_id(0)

    @pl.when(h == 0)
    def _():
        build_weights(pw_ref, order_ref, w_ref, layers)
        u_ref[...] = jnp.zeros_like(u_ref)

    residue = lax.axis_index("seq") * held + h
    window_rows(len_ref, lo_ref, hi_ref, residue, modulus)
    run_layers(x_ref.at[0], y_ref.at[0], gain_ref, bias_ref, taps_ref, w_ref, u_ref, act_ref, lo_ref, hi_ref, layers, shifts, modulus)


def local_stack(x, lengths, gains, biases, taps, pointwise, order, layers, shifts, modulus):
    held, rows, channels = x.shape
    pad = -(-max(shifts) // 8) * 8
    whole = lambda a: pl.BlockSpec(a.shape, lambda h: (0,) * a.ndim)
    order = order.reshape(order.shape[0], 1, channels)
    block = pl.BlockSpec((1, rows, channels), lambda h: (h, 0, 0))
    return pl.pallas_call(
        functools.partial(stack_kernel, layers, shifts, modulus, held),
        grid=(held,),
        out_shape=jax.ShapeDtypeStruct(x.shape, x.dtype),
        in_specs=[pl.BlockSpec(memory_space=pltpu.SMEM), block]
        + [whole(a) for a in (gains, biases, taps, pointwise, order)],
        out_specs=block,
        scratch_shapes=[
            pltpu.VMEM((len(layers), channels, channels), jnp.bfloat16),
            pltpu.VMEM((rows + 2 * pad, channels), jnp.float32),
            pltpu.VMEM((rows, channels), jnp.bfloat16),
            pltpu.VMEM((rows, LANES), jnp.int32),
            pltpu.VMEM((rows, LANES), jnp.int32),
        ],
        compiler_params=pltpu.CompilerParams(vmem_limit_bytes=48 * 2**20),
    )(lengths, x, gains, biases, taps, pointwise, order)


def halo_layer(stream, lengths, gain, bias, taps, weight, order, dilation):
    bins, channels = stream.shape
    count = lax.axis_size("seq")
    pos = lax.axis_index("seq") * bins + jnp.arange(bins, dtype=jnp.int32)
    ends = jnp.cumsum(lengths[0])
    passed = ends[None, :] <= pos[:, None]
    lo = jnp.max(jnp.where(passed, ends[None, :], 0), axis=-1)
    hi = jnp.min(jnp.where(passed, ends[-1], ends[None, :]), axis=-1)
    s = stream.astype(jnp.float32)
    inv = lax.rsqrt(jnp.mean(s * s, axis=-1, keepdims=True) + epsilon)
    normed = (s * inv * gain.astype(jnp.float32)).astype(jnp.bfloat16)
    before = lax.ppermute(normed[-dilation:], "seq", [(i, i + 1) for i in range(count - 1)])
    after = lax.ppermute(normed[:dilation], "seq", [(i + 1, i) for i in range(count - 1)])
    padded = jnp.concatenate([before, normed, after], axis=0).astype(jnp.float32)
    k = taps.astype(jnp.float32)
    v = k[1] * normed.astype(jnp.float32) + bias.astype(jnp.float32)
    v = v + k[0] * jnp.where((pos - dilation >= lo)[:, None], padded[:bins], 0.0)
    v = v + k[2] * jnp.where((pos + dilation < hi)[:, None], padded[2 * dilation :], 0.0)
    act = jax.nn.gelu(v, approximate=True).astype(jnp.bfloat16)
    width = weight.shape[-1]
    groups = channels // width
    projected = jnp.einsum(
        "ngi,gio->ngo",
        act.reshape(bins, groups, width),
        weight.reshape(groups, width, width),
        preferred_element_type=jnp.float32,
    ).reshape(bins, channels)
    return (s + jnp.take(projected, order, axis=-1)).astype(jnp.bfloat16)


def body(embedded, lengths, norm_gains, biases, conv_taps, pointwise, channel_order):
    _, bins, channels = embedded.shape
    layer_count = pointwise.shape[0]
    count = lax.axis_size("seq")
    dilations = [bins * 2**i // 2 ** (layer_count - 2) for i in range(layer_count)]
    modulus = max(count, dilations[0])
    stream = embedded[0]
    first = 0
    while dilations[first] % modulus:
        i = first
        stream = halo_layer(
            stream, lengths, norm_gains[i], biases[i], conv_taps[i], pointwise[i], channel_order[i], dilations[i]
        )
        first += 1
    layers = list(range(first, layer_count))
    shifts = [dilations[i] // modulus for i in layers]
    held = modulus // count
    per = bins // modulus
    x = stream.reshape(per, modulus, channels).transpose(1, 0, 2).reshape(count, held, per, channels)
    x = lax.all_to_all(x, "seq", 0, 0)
    x = x.transpose(1, 0, 2, 3).reshape(held, count * per, channels)
    y = local_stack(x, lengths, norm_gains, biases, conv_taps, pointwise, channel_order, layers, shifts, modulus)
    y = y.reshape(held, count, per, channels).transpose(1, 0, 2, 3)
    y = lax.all_to_all(y, "seq", 0, 0)
    y = y.reshape(modulus, per, channels).transpose(1, 0, 2)
    return y.reshape(1, bins, channels)


def solution(mesh):
    placed = (P("win", "seq", None), P("win", None), P(), P(), P(), P(), P())
    return jax.shard_map(
        body, mesh=mesh, in_specs=placed, out_specs=P("win", "seq", None), check_vma=False
    )
```

```python
import functools

import jax
import jax.numpy as jnp
from jax import lax
from jax.experimental import pallas as pl
from jax.experimental.pallas import tpu as pltpu
from jax.sharding import PartitionSpec as P

epsilon = 1e-06
LANES = 128
CHUNK = 128
MXU_ROWS = 256
GELU_C = 0.7978845608028654


def build_weights(pw_ref, order_ref, w_ref, layers):
    channels = w_ref.shape[-1]
    width = pw_ref.shape[-1]

    @pl.loop(0, len(layers))
    def _(i):
        layer = i + layers[0]
        order = order_ref[layer]
        for g in range(channels // width):
            out_ids = lax.broadcasted_iota(jnp.int32, (width, channels), 0) + g * width
            one_hot = jnp.where(out_ids == order, 1.0, 0.0).astype(jnp.bfloat16)
            rows = slice(g * width, (g + 1) * width)
            w_ref[i, rows, :] = jnp.dot(
                pw_ref[layer, rows, :], one_hot, preferred_element_type=jnp.float32
            ).astype(jnp.bfloat16)


def window_rows(len_ref, lo_ref, hi_ref, residue, modulus):
    rows = lo_ref.shape[0]
    pos = lax.broadcasted_iota(jnp.int32, (rows, LANES), 0) * modulus + residue
    wins = len_ref.shape[1]
    total = jnp.int32(0)
    for k in range(wins):
        total = total + len_ref[0, k]
    lo = jnp.zeros((rows, LANES), jnp.int32)
    hi = jnp.zeros((rows, LANES), jnp.int32) + total
    end = jnp.int32(0)
    ends = []
    for k in range(wins):
        end = end + len_ref[0, k]
        ends.append(end)
    for end in ends:
        lo = jnp.where(pos >= end, end, lo)
    for end in reversed(ends):
        hi = jnp.where(pos < end, end, hi)
    lo_ref[...] = pos - lo
    hi_ref[...] = hi - pos


def put_unit(u_ref, pad, start, size, stream):
    mean = jnp.mean(stream * stream, axis=-1, keepdims=True)
    u_ref[pl.ds(pad + start, size), :] = stream * lax.rsqrt(mean + epsilon)


def run_layers(x_ref, y_ref, gain_ref, bias_ref, taps_ref, w_ref, u_ref, act_ref, lo_ref, hi_ref, layers, shifts, modulus, copies):
    rows, channels = x_ref.shape
    pad = (u_ref.shape[0] - rows) // 2
    big = min(MXU_ROWS, rows)

    @pl.loop(0, rows // big)
    def _(i):
        start = pl.multiple_of(i * big, big)
        put_unit(u_ref, pad, start, big, x_ref[pl.ds(start, big), :].astype(jnp.float32))

    for i, layer in enumerate(layers):
        shift = shifts[i]
        source = x_ref if i == 0 else y_ref

        def mix(j, shift=shift, layer=layer):
            at = (lambda n: n) if isinstance(j, int) else (lambda n: pl.multiple_of(n, 8))
            start = j * CHUNK if isinstance(j, int) else pl.multiple_of(j * CHUNK, CHUNK)
            here = pl.ds(start, CHUNK)
            left_ok = lo_ref[here, :] >= shift * modulus
            right_ok = hi_ref[here, :] > shift * modulus
            for k in range(channels // LANES):
                cols = slice(k * LANES, (k + 1) * LANES)
                gain = gain_ref[layer : layer + 1, cols].astype(jnp.float32)
                tap = [gain * taps_ref[layer, t : t + 1, cols].astype(jnp.float32) for t in range(3)]
                bias = bias_ref[layer : layer + 1, cols].astype(jnp.float32)
                v = tap[1] * u_ref[pl.ds(at(start + pad), CHUNK), cols] + bias
                v = v + tap[0] * jnp.where(left_ok, u_ref[pl.ds(at(start + (pad - shift)), CHUNK), cols], 0.0)
                v = v + tap[2] * jnp.where(right_ok, u_ref[pl.ds(at(start + (pad + shift)), CHUNK), cols], 0.0)
                inner = v * (GELU_C + (GELU_C * 0.044715) * (v * v))
                half = 0.5 * v
                act_ref[here, cols] = (half + half * jnp.tanh(inner)).astype(jnp.bfloat16)

        if shift % 8:
            for j in range(rows // CHUNK):
                mix(j)
        else:
            pl.loop(0, rows // CHUNK)(mix)
        copies[i].wait()

        @pl.loop(0, rows // big)
        def _(j):
            start = pl.multiple_of(j * big, big)
            here = pl.ds(start, big)
            projected = jnp.dot(act_ref[here, :], w_ref[i], preferred_element_type=jnp.float32)
            fresh = (source[here, :].astype(jnp.float32) + projected).astype(jnp.bfloat16)
            y_ref[here, :] = fresh
            if i + 1 < len(layers):
                put_unit(u_ref, pad, start, big, fresh.astype(jnp.float32))


def weights_kernel(layers, pw_ref, order_ref, w_ref):
    build_weights(pw_ref, order_ref, w_ref, layers)


def dense_weights(pointwise, order, layers):
    channels = pointwise.shape[1]
    in_vmem = pl.BlockSpec(memory_space=pltpu.VMEM)
    return pl.pallas_call(
        functools.partial(weights_kernel, layers),
        out_shape=jax.ShapeDtypeStruct((len(layers), channels, channels), pointwise.dtype),
        in_specs=[in_vmem] * 2,
        out_specs=in_vmem,
        cost_estimate=pl.CostEstimate(flops=2 * 10**9, bytes_accessed=2 * 10**7, transcendentals=0),
        compiler_params=pltpu.CompilerParams(vmem_limit_bytes=12 * 2**20),
    )(pointwise, order.reshape(order.shape[0], 1, channels))


def stack_kernel(layers, shifts, modulus, base, len_ref, x_ref, gain_ref, bias_ref, taps_ref, w_hbm, y_ref, u_ref, act_ref, lo_ref, hi_ref, w_ref, sems):
    copies = [pltpu.make_async_copy(w_hbm.at[i], w_ref.at[i], sems.at[i]) for i in range(len(layers))]
    for copy in copies:
        copy.start()
    pad = (u_ref.shape[0] - x_ref.shape[0]) // 2
    edge = jnp.zeros((pad, u_ref.shape[1]), u_ref.dtype)
    u_ref[:pad, :] = edge
    u_ref[u_ref.shape[0] - pad :, :] = edge
    window_rows(len_ref, lo_ref, hi_ref, lax.axis_index("seq") + base, modulus)
    run_layers(x_ref, y_ref, gain_ref, bias_ref, taps_ref, w_ref, u_ref, act_ref, lo_ref, hi_ref, layers, shifts, modulus, copies)


def local_stack(x, lengths, gains, biases, taps, weights, layers, shifts, modulus, base):
    rows, channels = x.shape
    pad = -(-max(shifts) // 8) * 8
    in_vmem = pl.BlockSpec(memory_space=pltpu.VMEM)
    return pl.pallas_call(
        functools.partial(stack_kernel, layers, shifts, modulus, base),
        out_shape=jax.ShapeDtypeStruct(x.shape, x.dtype),
        in_specs=[pl.BlockSpec(memory_space=pltpu.SMEM)] + [in_vmem] * 4 + [pl.BlockSpec(memory_space=pltpu.HBM)],
        out_specs=in_vmem,
        scratch_shapes=[
            pltpu.VMEM((rows + 2 * pad, channels), jnp.float32),
            pltpu.VMEM((rows, channels), jnp.bfloat16),
            pltpu.VMEM((rows, LANES), jnp.int32),
            pltpu.VMEM((rows, LANES), jnp.int32),
            pltpu.VMEM(weights.shape, weights.dtype),
            pltpu.SemaphoreType.DMA((len(layers),)),
        ],
        cost_estimate=pl.CostEstimate(flops=2 * 10**10, bytes_accessed=2 * 10**7, transcendentals=0),
        compiler_params=pltpu.CompilerParams(vmem_limit_bytes=56 * 2**20),
    )(lengths, x, gains, biases, taps, weights)


def halo_layer(stream, lengths, gain, bias, taps, weight, order, dilation):
    bins, channels = stream.shape
    count = lax.axis_size("seq")
    pos = lax.axis_index("seq") * bins + jnp.arange(bins, dtype=jnp.int32)
    ends = jnp.cumsum(lengths[0])
    passed = ends[None, :] <= pos[:, None]
    lo = jnp.max(jnp.where(passed, ends[None, :], 0), axis=-1)
    hi = jnp.min(jnp.where(passed, ends[-1], ends[None, :]), axis=-1)
    s = stream.astype(jnp.float32)
    inv = lax.rsqrt(jnp.mean(s * s, axis=-1, keepdims=True) + epsilon)
    normed = (s * inv * gain.astype(jnp.float32)).astype(jnp.bfloat16)
    before = lax.ppermute(normed[-dilation:], "seq", [(i, i + 1) for i in range(count - 1)])
    after = lax.ppermute(normed[:dilation], "seq", [(i + 1, i) for i in range(count - 1)])
    padded = jnp.concatenate([before, normed, after], axis=0).astype(jnp.float32)
    k = taps.astype(jnp.float32)
    v = k[1] * normed.astype(jnp.float32) + bias.astype(jnp.float32)
    v = v + k[0] * jnp.where((pos - dilation >= lo)[:, None], padded[:bins], 0.0)
    v = v + k[2] * jnp.where((pos + dilation < hi)[:, None], padded[2 * dilation :], 0.0)
    act = jax.nn.gelu(v, approximate=True).astype(jnp.bfloat16)
    width = weight.shape[-1]
    groups = channels // width
    projected = jnp.einsum(
        "ngi,gio->ngo",
        act.reshape(bins, groups, width),
        weight.reshape(groups, width, width),
        preferred_element_type=jnp.float32,
    ).reshape(bins, channels)
    return (s + jnp.take(projected, order, axis=-1)).astype(jnp.bfloat16)


def body(embedded, lengths, norm_gains, biases, conv_taps, pointwise, channel_order):
    _, bins, channels = embedded.shape
    layer_count = pointwise.shape[0]
    count = lax.axis_size("seq")
    dilations = [bins * 2**i // 2 ** (layer_count - 2) for i in range(layer_count)]
    modulus = max(count, dilations[0])
    stream = embedded[0]
    first = 0
    while dilations[first] % modulus:
        i = first
        stream = halo_layer(
            stream, lengths, norm_gains[i], biases[i], conv_taps[i], pointwise[i], channel_order[i], dilations[i]
        )
        first += 1
    layers = list(range(first, layer_count))
    shifts = [dilations[i] // modulus for i in layers]
    held = modulus // count
    per = bins // modulus
    weights = dense_weights(pointwise, channel_order, layers)
    spread = stream.reshape(per, modulus, channels)
    back = []
    arrived = None
    for h in range(held):
        part = spread[:, h * count : (h + 1) * count].transpose(1, 0, 2)
        if arrived is not None:
            part, arrived = lax.optimization_barrier((part, arrived))
            back.append(arrived)
        arrived = lax.all_to_all(part, "seq", 0, 0)
    back.append(arrived)
    done = None
    outs = []
    for h in range(held):
        x = back[h].reshape(count * per, channels)
        if done is not None:
            outs.append(lax.all_to_all(done.reshape(count, per, channels), "seq", 0, 0))
        done = local_stack(x, lengths, norm_gains, biases, conv_taps, weights, layers, shifts, modulus, h * count)
    outs.append(lax.all_to_all(done.reshape(count, per, channels), "seq", 0, 0))
    y = jnp.concatenate([o.transpose(1, 0, 2) for o in outs], axis=1)
    return y.reshape(1, bins, channels)


def solution(mesh):
    placed = (P("win", "seq", None), P("win", None), P(), P(), P(), P(), P())
    return jax.shard_map(
        body, mesh=mesh, in_specs=placed, out_specs=P("win", "seq", None), check_vma=False
    )
```

```python
import functools

import jax
import jax.numpy as jnp
from jax import lax
from jax.experimental import pallas as pl
from jax.experimental.pallas import tpu as pltpu
from jax.sharding import PartitionSpec as P

epsilon = 1e-06
LANES = 128
CHUNK = 128
MXU_ROWS = 256
GELU_C = 0.7978845608028654


def build_weights(pw_ref, order_ref, w_ref, layers):
    channels = w_ref.shape[-1]
    width = pw_ref.shape[-1]

    @pl.loop(0, len(layers))
    def _(i):
        layer = i + layers[0]
        order = order_ref[layer]
        for g in range(channels // width):
            out_ids = lax.broadcasted_iota(jnp.int32, (width, channels), 0) + g * width
            one_hot = jnp.where(out_ids == order, 1.0, 0.0).astype(jnp.bfloat16)
            rows = slice(g * width, (g + 1) * width)
            w_ref[i, rows, :] = jnp.dot(
                pw_ref[layer, rows, :], one_hot, preferred_element_type=jnp.float32
            ).astype(jnp.bfloat16)


def window_rows(len_ref, lo_ref, hi_ref, residue, modulus):
    rows = lo_ref.shape[0]
    pos = lax.broadcasted_iota(jnp.int32, (rows, LANES), 0) * modulus + residue
    wins = len_ref.shape[1]
    total = jnp.int32(0)
    for k in range(wins):
        total = total + len_ref[0, k]
    lo = jnp.zeros((rows, LANES), jnp.int32)
    hi = jnp.zeros((rows, LANES), jnp.int32) + total
    end = jnp.int32(0)
    ends = []
    for k in range(wins):
        end = end + len_ref[0, k]
        ends.append(end)
    for end in ends:
        lo = jnp.where(pos >= end, end, lo)
    for end in reversed(ends):
        hi = jnp.where(pos < end, end, hi)
    lo_ref[...] = pos - lo
    hi_ref[...] = hi - pos


def put_unit(u_ref, pad, start, size, stream):
    mean = jnp.mean(stream * stream, axis=-1, keepdims=True)
    u_ref[pl.ds(pad + start, size), :] = stream * lax.rsqrt(mean + epsilon)


def run_layers(x_ref, y_ref, gain_ref, bias_ref, taps_ref, w_ref, u_ref, act_ref, lo_ref, hi_ref, layers, shifts, modulus, copies):
    rows, channels = x_ref.shape
    pad = (u_ref.shape[1] - rows) // 2
    big = min(MXU_ROWS, rows)
    straight = rows <= 2 * MXU_ROWS

    @pl.loop(0, rows // big)
    def _(i):
        start = pl.multiple_of(i * big, big)
        put_unit(u_ref.at[0], pad, start, big, x_ref[pl.ds(start, big), :].astype(jnp.float32))

    for i, layer in enumerate(layers):
        shift = shifts[i]
        source = x_ref if i == 0 else y_ref
        now, later = u_ref.at[i % 2], u_ref.at[(i + 1) % 2]

        def mix(j, shift=shift, layer=layer, now=now):
            at = (lambda n: n) if isinstance(j, int) else (lambda n: pl.multiple_of(n, 8))
            start = j * CHUNK if isinstance(j, int) else pl.multiple_of(j * CHUNK, CHUNK)
            here = pl.ds(start, CHUNK)
            left_ok = lo_ref[here, :] >= shift * modulus
            right_ok = hi_ref[here, :] > shift * modulus
            for k in range(channels // LANES):
                cols = slice(k * LANES, (k + 1) * LANES)
                gain = gain_ref[layer : layer + 1, cols].astype(jnp.float32)
                tap = [gain * taps_ref[layer, t : t + 1, cols].astype(jnp.float32) for t in range(3)]
                bias = bias_ref[layer : layer + 1, cols].astype(jnp.float32)
                v = tap[1] * now[pl.ds(at(start + pad), CHUNK), cols] + bias
                v = v + tap[0] * jnp.where(left_ok, now[pl.ds(at(start + (pad - shift)), CHUNK), cols], 0.0)
                v = v + tap[2] * jnp.where(right_ok, now[pl.ds(at(start + (pad + shift)), CHUNK), cols], 0.0)
                inner = v * (GELU_C + (GELU_C * 0.044715) * (v * v))
                half = 0.5 * v
                act_ref[here, cols] = (half + half * jnp.tanh(inner)).astype(jnp.bfloat16)

        def project(j, i=i, source=source, later=later):
            start = j * big if isinstance(j, int) else pl.multiple_of(j * big, big)
            here = pl.ds(start, big)
            projected = jnp.dot(act_ref[here, :], w_ref[i], preferred_element_type=jnp.float32)
            fresh = (source[here, :].astype(jnp.float32) + projected).astype(jnp.bfloat16)
            y_ref[here, :] = fresh
            if i + 1 < len(layers):
                put_unit(later, pad, start, big, fresh.astype(jnp.float32))

        copies[i].wait()
        if straight:
            for j in range(rows // big):
                for k in range(big // CHUNK):
                    mix(j * (big // CHUNK) + k)
                project(j)
        else:
            if shift % 8:
                for j in range(rows // CHUNK):
                    mix(j)
            else:
                pl.loop(0, rows // CHUNK)(mix)
            pl.loop(0, rows // big)(project)


def weights_kernel(layers, pw_ref, order_ref, w_ref):
    build_weights(pw_ref, order_ref, w_ref, layers)


def dense_weights(pointwise, order, layers):
    channels = pointwise.shape[1]
    in_vmem = pl.BlockSpec(memory_space=pltpu.VMEM)
    return pl.pallas_call(
        functools.partial(weights_kernel, layers),
        out_shape=jax.ShapeDtypeStruct((len(layers), channels, channels), pointwise.dtype),
        in_specs=[in_vmem] * 2,
        out_specs=in_vmem,
        cost_estimate=pl.CostEstimate(flops=2 * 10**9, bytes_accessed=2 * 10**7, transcendentals=0),
        compiler_params=pltpu.CompilerParams(vmem_limit_bytes=12 * 2**20),
    )(pointwise, order.reshape(order.shape[0], 1, channels))


def stack_kernel(layers, shifts, modulus, base, len_ref, x_ref, gain_ref, bias_ref, taps_ref, w_hbm, y_ref, u_ref, act_ref, lo_ref, hi_ref, w_ref, sems):
    copies = [pltpu.make_async_copy(w_hbm.at[i], w_ref.at[i], sems.at[i]) for i in range(len(layers))]
    for copy in copies:
        copy.start()
    pad = (u_ref.shape[1] - x_ref.shape[0]) // 2
    edge = jnp.zeros((2, pad, u_ref.shape[2]), u_ref.dtype)
    u_ref[:, :pad, :] = edge
    u_ref[:, u_ref.shape[1] - pad :, :] = edge
    window_rows(len_ref, lo_ref, hi_ref, lax.axis_index("seq") + base, modulus)
    run_layers(x_ref, y_ref, gain_ref, bias_ref, taps_ref, w_ref, u_ref, act_ref, lo_ref, hi_ref, layers, shifts, modulus, copies)


def local_stack(x, lengths, gains, biases, taps, weights, layers, shifts, modulus, base):
    rows, channels = x.shape
    pad = -(-max(shifts) // 8) * 8
    in_vmem = pl.BlockSpec(memory_space=pltpu.VMEM)
    return pl.pallas_call(
        functools.partial(stack_kernel, layers, shifts, modulus, base),
        out_shape=jax.ShapeDtypeStruct(x.shape, x.dtype),
        in_specs=[pl.BlockSpec(memory_space=pltpu.SMEM)] + [in_vmem] * 4 + [pl.BlockSpec(memory_space=pltpu.HBM)],
        out_specs=in_vmem,
        scratch_shapes=[
            pltpu.VMEM((2, rows + 2 * pad, channels), jnp.float32),
            pltpu.VMEM((rows, channels), jnp.bfloat16),
            pltpu.VMEM((rows, LANES), jnp.int32),
            pltpu.VMEM((rows, LANES), jnp.int32),
            pltpu.VMEM(weights.shape, weights.dtype),
            pltpu.SemaphoreType.DMA((len(layers),)),
        ],
        cost_estimate=pl.CostEstimate(flops=2 * 10**10, bytes_accessed=2 * 10**7, transcendentals=0),
        compiler_params=pltpu.CompilerParams(vmem_limit_bytes=56 * 2**20),
    )(lengths, x, gains, biases, taps, weights)


def halo_layer(stream, lengths, gain, bias, taps, weight, order, dilation):
    bins, channels = stream.shape
    count = lax.axis_size("seq")
    pos = lax.axis_index("seq") * bins + jnp.arange(bins, dtype=jnp.int32)
    ends = jnp.cumsum(lengths[0])
    passed = ends[None, :] <= pos[:, None]
    lo = jnp.max(jnp.where(passed, ends[None, :], 0), axis=-1)
    hi = jnp.min(jnp.where(passed, ends[-1], ends[None, :]), axis=-1)
    s = stream.astype(jnp.float32)
    inv = lax.rsqrt(jnp.mean(s * s, axis=-1, keepdims=True) + epsilon)
    normed = (s * inv * gain.astype(jnp.float32)).astype(jnp.bfloat16)
    before = lax.ppermute(normed[-dilation:], "seq", [(i, i + 1) for i in range(count - 1)])
    after = lax.ppermute(normed[:dilation], "seq", [(i + 1, i) for i in range(count - 1)])
    padded = jnp.concatenate([before, normed, after], axis=0).astype(jnp.float32)
    k = taps.astype(jnp.float32)
    v = k[1] * normed.astype(jnp.float32) + bias.astype(jnp.float32)
    v = v + k[0] * jnp.where((pos - dilation >= lo)[:, None], padded[:bins], 0.0)
    v = v + k[2] * jnp.where((pos + dilation < hi)[:, None], padded[2 * dilation :], 0.0)
    act = jax.nn.gelu(v, approximate=True).astype(jnp.bfloat16)
    width = weight.shape[-1]
    groups = channels // width
    projected = jnp.einsum(
        "ngi,gio->ngo",
        act.reshape(bins, groups, width),
        weight.reshape(groups, width, width),
        preferred_element_type=jnp.float32,
    ).reshape(bins, channels)
    return (s + jnp.take(projected, order, axis=-1)).astype(jnp.bfloat16)


def body(embedded, lengths, norm_gains, biases, conv_taps, pointwise, channel_order):
    _, bins, channels = embedded.shape
    layer_count = pointwise.shape[0]
    count = lax.axis_size("seq")
    dilations = [bins * 2**i // 2 ** (layer_count - 2) for i in range(layer_count)]
    modulus = max(count, dilations[0])
    stream = embedded[0]
    first = 0
    while dilations[first] % modulus:
        i = first
        stream = halo_layer(
            stream, lengths, norm_gains[i], biases[i], conv_taps[i], pointwise[i], channel_order[i], dilations[i]
        )
        first += 1
    layers = list(range(first, layer_count))
    shifts = [dilations[i] // modulus for i in layers]
    held = modulus // count
    per = bins // modulus
    weights = dense_weights(pointwise, channel_order, layers)
    spread = stream.reshape(per, modulus, channels)
    back = []
    arrived = None
    for h in range(held):
        part = spread[:, h * count : (h + 1) * count].transpose(1, 0, 2)
        if arrived is not None:
            part, arrived = lax.optimization_barrier((part, arrived))
            back.append(arrived)
        arrived = lax.all_to_all(part, "seq", 0, 0)
    back.append(arrived)
    done = None
    outs = []
    for h in range(held):
        x = back[h].reshape(count * per, channels)
        if done is not None:
            outs.append(lax.all_to_all(done.reshape(count, per, channels), "seq", 0, 0))
        done = local_stack(x, lengths, norm_gains, biases, conv_taps, weights, layers, shifts, modulus, h * count)
    outs.append(lax.all_to_all(done.reshape(count, per, channels), "seq", 0, 0))
    y = jnp.concatenate([o.transpose(1, 0, 2) for o in outs], axis=1)
    return y.reshape(1, bins, channels)


def solution(mesh):
    placed = (P("win", "seq", None), P("win", None), P(), P(), P(), P(), P())
    return jax.shard_map(
        body, mesh=mesh, in_specs=placed, out_specs=P("win", "seq", None), check_vma=False
    )
```
